256 devices in a mesh: corpus: 32 (over z_lo, x, core), query: 8 (over z_hi, y).
Axes of the slice: x: 4, y: 4, z: 8 (z_hi: 2, z_lo: 4; z = z_hi * 4 + z_lo), core: 2. Of those that a mesh axis runs over, the one named last changes fastest.
Arguments:
- inputs: bfloat16 [131072, 4096], P(('corpus', 'query'))
- cotangents: bfloat16 [131072, 4096], P(('corpus', 'query')), may hold values from -6 to 6
- sketch_maps: bfloat16 [4096, 128], replicated, may hold values from -0.09375 to 0.09375
- lengths: int32 [1024], P(('corpus', 'query')), may hold values from 1 to 128, 81920 in all
- queries: bfloat16 [2048, 4096], P(('query', 'corpus')), may hold values from -0.09375 to 0.09375
Outputs:
- scores: float32 [131072, 2048], P('corpus', 'query')
The draws below stay inside these ranges and needn't reach their ends.
Inputs may be any that keep to these rules, and one draw needn't show every extreme that they name: `lengths`: each training sequence has at least one live token; some sequence has 128.
All inputs are finite; a program needn't handle non-finite values. No bound on the sum of `lengths` on one device may be relied on, other than what follows from the above.
Results may differ from the reference program's by a relative error of at most 0.005.
Values may be sent and summed in bfloat16 or wider, within the bound.
No kernel may reach another device: no remote copies, remote signals or barrier semaphores. Data moves between devices by JAX's collectives and lax.ppermute only.
A program may use at most 128 MiB of HBM per device.

```python
import math
import jax
import jax.numpy as jnp
import numpy as np
from jax import lax

D = 4096
R = 64
LEN = 128
SEQ_DEV = 4
SEQS = 1024
TOKENS = 131072
Q = 2048


def draw_inputs(key, part):
    key = jax.random.fold_in(key, 11)
    scale_key, value_key = jax.random.split(key, 2)
    position = jnp.arange(TOKENS, dtype=jnp.float32) / TOKENS
    row_scale = (1.0 + 2.0 * position) * jnp.exp(jax.random.uniform(scale_key, (TOKENS,), jnp.float32, -0.7, 0.7))
    values = jax.random.normal(value_key, (TOKENS, D), jnp.float32)
    return (values * row_scale[:, None]).astype(jnp.bfloat16)


def shard_levels(key, shape, shards, smallest, high):
    level = 1.0
    for dim, parts in shards:
        steps = jax.random.uniform(jax.random.fold_in(jax.random.fold_in(key, 6), dim), (parts,), jnp.float32, smallest / len(shards), high / len(shards))
        level = level * jnp.repeat(jnp.exp(steps), shape[dim] // parts).reshape((-1,) + (1,) * (len(shape) - 1 - dim))
    return level


def split_up(number_of, total, most, lean):
    weights = [(1 << 20) // math.isqrt(rank ** lean) + 1 for rank in range(2, number_of + 1)]
    surplus, given = total - most - (number_of - 1), [1] * (number_of - 1)
    while surplus > 0:
        free = [i for i in range(number_of - 1) if given[i] < most]
        whole, budget = sum([weights[i] for i in free]), surplus
        for i in free:
            addition = min(most - given[i], max(1, budget * weights[i] // whole), surplus)
            given[i] = given[i] + addition
            surplus = surplus - addition
    return np.array([most] + given)


def uneven(own_key, number_of, total, bound, slope):
    if number_of == 2:
        one = jax.random.randint(own_key, (), max(1, total - bound), min(bound, total - 1) + 1)
        return jnp.stack([one, total - one])
    sizes = jnp.asarray(split_up(number_of, total, bound, slope), jnp.int32)
    couples = (number_of - 1) // 2
    donor, taker = sizes[1:1 + 2 * couples:2], sizes[2:2 + 2 * couples:2]
    margin = jnp.minimum(donor - 1, bound - taker)
    moved = jax.random.randint(jax.random.fold_in(own_key, 1), (couples,), 0, 1 << 20) % (margin + 1)
    sizes = sizes.at[1:1 + 2 * couples:2].set(donor - moved).at[2:2 + 2 * couples:2].set(taker + moved)
    return sizes[jax.random.permutation(jax.random.fold_in(own_key, 2), number_of)]


def noise(stream_key, dims, scale, reach, pieces=(), kind=jnp.bfloat16):
    gain = shard_levels(stream_key, dims, pieces, -0.22, 0.18) if pieces else 1.0
    result = jax.random.normal(stream_key, dims, jnp.float32) * scale * gain
    return jnp.minimum(jnp.maximum(result, -reach), reach).astype(kind)


def setup_inputs(seed: int = 0) -> dict:
    key_of = jax.random.split(jax.random.key(seed), 6)
    return {
        "inputs": draw_inputs(jax.random.fold_in(key_of[5], 71), 0),
        "cotangents": noise(key_of[1], (TOKENS, D), 1.0, 6.0, ((0, 256),)),
        "sketch_maps": noise(key_of[2], (D, 2 * R), D ** -0.5, 0.09375),
        "lengths": uneven(key_of[3], SEQS, SEQS * LEN * 5 // 8, LEN, 2).astype(jnp.int32),
        "queries": noise(key_of[4], (Q, R * R), (R * R) ** -0.5, 0.09375, ((0, 256),)),
    }


def damped_inverse(moment):
    size = moment.shape[0]
    identity = jnp.eye(size, dtype=jnp.float32)
    damped = moment + 0.1 * jnp.trace(moment) / size * identity
    factor = jnp.linalg.cholesky(damped)
    return jax.scipy.linalg.cho_solve((factor, True), identity)

def condition(query_block, inverse_out, inverse_in):
    number = query_block.shape[0]
    size = inverse_in.shape[0]
    matrices = query_block.astype(jnp.float32).reshape(number, size, size)
    left = jnp.einsum('ik,qkj->qij', inverse_out, matrices, precision=lax.Precision.HIGHEST)
    both = jnp.einsum('qik,kj->qij', left, inverse_in, precision=lax.Precision.HIGHEST)
    return both.reshape(number, size * size).astype(jnp.bfloat16)

def reference(inputs, cotangents, sketch_maps, lengths, queries):
    live_mask = (jnp.arange(LEN, dtype=jnp.int32)[None, :] < lengths[:, None]).reshape(-1).astype(jnp.float32)
    side_in = jnp.dot(inputs.astype(jnp.float32), sketch_maps[:, :R].astype(jnp.float32), preferred_element_type=jnp.float32) * live_mask[:, None]
    side_out = jnp.dot(cotangents.astype(jnp.float32), sketch_maps[:, R:].astype(jnp.float32), preferred_element_type=jnp.float32) * live_mask[:, None]
    counted = jnp.sum(live_mask)
    moment_in = jnp.dot(side_in.T, side_in, precision=lax.Precision.HIGHEST) / counted
    moment_out = jnp.dot(side_out.T, side_out, precision=lax.Precision.HIGHEST) / counted
    conditioned = condition(queries, damped_inverse(moment_out), damped_inverse(moment_in))
    block_rows = SEQ_DEV * LEN

    def score_block(sides):
        block_in, block_out = sides
        sketch = (block_out[:, :, None] * block_in[:, None, :]).reshape(block_rows, R * R).astype(jnp.bfloat16)
        return lax.dot_general(sketch.astype(jnp.float32), conditioned.astype(jnp.float32), (((1,), (1,)), ((), ())), preferred_element_type=jnp.float32)
    blocks = lax.map(score_block, (side_in.reshape(-1, block_rows, R), side_out.reshape(-1, block_rows, R)))
    return blocks.reshape(TOKENS, Q)
```

```python
import functools

import jax
import jax.numpy as jnp
from jax import lax
from jax.experimental import pallas as pl
from jax.experimental.pallas import tpu as pltpu
from jax.sharding import PartitionSpec as P

F32 = jnp.float32
BF16 = jnp.bfloat16
BOTH = ("corpus", "query")
NT = (((1,), (1,)), ((), ()))
TN = (((0,), (0,)), ((), ()))
MIB = 1 << 20


def exchange(array, corpus_bits, query_bits):
    pairs = [
        (c * 8 + q, (c ^ corpus_bits) * 8 + (q ^ query_bits))
        for c in range(32)
        for q in range(8)
    ]
    return lax.ppermute(array, BOTH, pairs)


def along_z(array, partner):
    pairs = []
    for c in range(32):
        for q in range(8):
            z = partner[(q >> 2) * 4 + (c >> 3)]
            pairs.append((c * 8 + q, ((z & 3) * 8 + (c & 7)) * 8 + (z >> 2) * 4 + (q & 3)))
    return lax.ppermute(array, BOTH, pairs)


def sum_over_all(part):
    part = part + exchange(part, 1, 0)
    part = part + exchange(part, 2, 0)
    part = part + exchange(part, 6, 0)
    part = part + exchange(part, 0, 1)
    part = part + exchange(part, 0, 3)
    part = part + along_z(part, (1, 0, 3, 2, 5, 4, 7, 6))
    part = part + along_z(part, (7, 2, 1, 4, 3, 6, 5, 0))
    return part + along_z(part, (3, 6, 5, 0, 7, 2, 1, 4))


def sides_kernel(lengths_ref, inputs_ref, cotangents_ref, maps_ref, sides_ref, sums_ref):
    step = pl.program_id(0)
    rank = maps_ref.shape[1] // 2
    rows = inputs_ref.shape[0]
    maps = maps_ref[...]
    of_in = jnp.dot(inputs_ref[...], maps, preferred_element_type=F32)
    of_out = jnp.dot(cotangents_ref[...], maps, preferred_element_type=F32)
    lane = lax.broadcasted_iota(jnp.int32, of_in.shape, 1)
    row = lax.broadcasted_iota(jnp.int32, of_in.shape, 0)
    length = lengths_ref[step]
    sides = jnp.where(row < length, jnp.where(lane < rank, of_in, of_out), 0.0)
    sides_ref[...] = sides.astype(BF16)
    gram = lax.dot_general(sides, sides, TN, precision=lax.Precision.HIGHEST, preferred_element_type=F32)
    half = lax.broadcasted_iota(jnp.int32, (rank, 2 * rank), 1) < rank

    @pl.when(step == 0)
    def _():
        sums_ref[...] = jnp.zeros_like(sums_ref)

    sums_ref[:rank, :] += jnp.where(half, gram[:rank], gram[rank:])
    sums_ref[rank:, :] += jnp.full((8, 2 * rank), 1.0, F32) * length.astype(F32)


def sides_and_sums(inputs, cotangents, sketch_maps, lengths):
    rows, width = inputs.shape
    sequences = lengths.shape[0]
    slots = rows // sequences
    both = sketch_maps.shape[1]
    return pl.pallas_call(
        sides_kernel,
        grid_spec=pltpu.PrefetchScalarGridSpec(
            num_scalar_prefetch=1,
            grid=(sequences,),
            in_specs=[
                pl.BlockSpec((slots, width), lambda i, n: (i, 0)),
                pl.BlockSpec((slots, width), lambda i, n: (i, 0)),
                pl.BlockSpec((width, both), lambda i, n: (0, 0)),
            ],
            out_specs=[
                pl.BlockSpec((slots, both), lambda i, n: (i, 0)),
                pl.BlockSpec((both // 2 + 8, both), lambda i, n: (0, 0)),
            ],
        ),
        out_shape=[
            jax.ShapeDtypeStruct((rows, both), BF16),
            jax.ShapeDtypeStruct((both // 2 + 8, both), F32),
        ],
        compiler_params=pltpu.CompilerParams(vmem_limit_bytes=24 * MIB),
        cost_estimate=pl.CostEstimate(
            flops=4 * rows * width * both, bytes_accessed=4 * rows * width, transcendentals=0
        ),
    )(lengths, inputs, cotangents, sketch_maps)


def damped_inverses(sums):
    rank = sums.shape[0] - 8
    shape = (rank, 2 * rank)
    row = lax.broadcasted_iota(jnp.int32, shape, 0)
    lane = lax.broadcasted_iota(jnp.int32, shape, 1)
    left = lane < rank
    column = jnp.where(left, lane, lane - rank)
    moment = sums[:rank] / sums[rank : rank + 1]
    diagonal = jnp.where(row == column, moment, 0.0)
    trace_in = jnp.sum(jnp.where(left, diagonal, 0.0))
    trace_out = jnp.sum(jnp.where(left, 0.0, diagonal))
    damping = 0.1 / rank * jnp.where(left, trace_in, trace_out)
    work = moment + jnp.where(row == column, damping, 0.0)
    for k in range(rank):
        pivot_column = jnp.where(left, work[:, k : k + 1], work[:, rank + k : rank + k + 1])
        at_column = column == k
        inverse = 1.0 / pivot_column[k : k + 1]
        pivot_row = jnp.where(at_column[:1], 1.0, work[k : k + 1]) * inverse
        swept = jnp.where(at_column, 0.0, work) - pivot_column * pivot_row
        work = jnp.where(row == k, pivot_row, swept)
    return work


def scores_kernel(place_ref, sums_ref, near_ref, far_ref, *rest, tile):
    *parts, out_ref, held, blocks, first, second, lhs, turned, moved, sem = rest
    step, steps = pl.program_id(0), pl.num_programs(0)
    rank = sums_ref.shape[0] - 8
    near = near_ref.shape[0]
    part = parts[0].shape[0]

    def build(index, into):
        sides = blocks[pl.ds(pl.multiple_of(index * tile, tile), tile), :]
        turned[...] = lax.dot_general(lhs[0], sides, NT, preferred_element_type=F32) + lax.dot_general(
            lhs[1], sides, NT, preferred_element_type=F32
        )
        of_in = turned[:rank, :]
        for i in range(rank):
            into[i * rank : (i + 1) * rank, :] = (turned[rank + i : rank + i + 1, :] * of_in).astype(BF16)

    def score(sketch, half):
        product = jnp.dot(held[...], sketch[...], preferred_element_type=F32)
        for slot in range(product.shape[0] // 8):
            difference = (slot & 3) * 8 + ((slot >> 2) & 3) * 2 + (slot >> 4)
            target = pl.multiple_of((place_ref[0] ^ difference) * 8, 8)
            moved[pl.ds(target, 8), :] = product[slot * 8 : (slot + 1) * 8, :]
        out_ref[half * tile : (half + 1) * tile, :] = moved[...].T

    @pl.when(step == 0)
    def _():
        copies = [
            pltpu.make_async_copy(near_ref, held.at[pl.ds(0, near), :], sem.at[0]),
            pltpu.make_async_copy(far_ref, held.at[pl.ds(near, near), :], sem.at[1]),
        ]
        for i, ref in enumerate(parts):
            copies.append(pltpu.make_async_copy(ref, blocks.at[pl.ds(i * part, part), :], sem.at[2 + i]))
        for copy in copies:
            copy.start()
        inverses = damped_inverses(sums_ref[...])
        left = lax.broadcasted_iota(jnp.int32, inverses.shape, 1) < rank
        whole = jnp.concatenate([jnp.where(left, inverses, 0.0), jnp.where(left, 0.0, inverses)])
        high = whole.astype(BF16)
        lhs[0] = high
        lhs[1] = (whole - high.astype(F32)).astype(BF16)
        for copy in copies:
            copy.wait()
        build(0, first)

    score(first, 0)
    build(2 * step + 1, second)
    score(second, 1)
    build(jnp.minimum(2 * step + 2, 2 * steps - 2), first)


def scores_of(place, sums, near, far, parts, tile=256):
    both = sums.shape[1]
    number, entries = 2 * near.shape[0], near.shape[1]
    rows = sum(part.shape[0] for part in parts)
    steps = rows // (2 * tile)
    anywhere = pl.BlockSpec(memory_space=pl.ANY)
    return pl.pallas_call(
        functools.partial(scores_kernel, tile=tile),
        grid_spec=pltpu.PrefetchScalarGridSpec(
            num_scalar_prefetch=1,
            grid=(steps,),
            in_specs=[pl.BlockSpec(sums.shape, lambda i, p: (0, 0))] + [anywhere] * (2 + len(parts)),
            out_specs=pl.BlockSpec(
                (2 * tile, number), lambda i, p: (p[1] ^ ((i & 1) * 4 + (i >> 1)), 0)
            ),
            scratch_shapes=[
                pltpu.VMEM((number, entries), BF16),
                pltpu.VMEM((rows, both), BF16),
                pltpu.VMEM((entries, tile), BF16),
                pltpu.VMEM((entries, tile), BF16),
                pltpu.VMEM((2, both, both), BF16),
                pltpu.VMEM((both, tile), F32),
                pltpu.VMEM((number, tile), F32),
                pltpu.SemaphoreType.DMA((2 + len(parts),)),
            ],
        ),
        out_shape=jax.ShapeDtypeStruct((rows, number), F32),
        compiler_params=pltpu.CompilerParams(vmem_limit_bytes=32 * MIB),
        cost_estimate=pl.CostEstimate(
            flops=2 * rows * number * entries, bytes_accessed=4 * rows * number, transcendentals=0
        ),
    )(place, sums, near, far, *parts)


def shards(inputs, cotangents, sketch_maps, lengths, queries):
    line = jnp.concatenate([queries] + [exchange(queries, 8 * d, 0) for d in (1, 2, 3)])
    near = jnp.concatenate([line] + [exchange(line, 2 * d, 0) for d in (1, 2, 3)])
    far = exchange(near, 1, 0)
    sides, part = sides_and_sums(inputs, cotangents, sketch_maps, lengths)
    pair = jnp.concatenate([sides, exchange(sides, 0, 4)])
    parts = [pair] + [exchange(pair, 0, d) for d in (1, 2, 3)]
    sums = sum_over_all(part)
    place = jnp.stack([lax.axis_index("corpus"), lax.axis_index("query")]).astype(jnp.int32)
    return scores_of(place, sums, near, far, parts)


def solution(mesh):
    placed = (
        P(BOTH, None),
        P(BOTH, None),
        P(),
        P(BOTH),
        P(("query", "corpus"), None),
    )
    return jax.shard_map(
        shards, mesh=mesh, in_specs=placed, out_specs=P("corpus", "query"), check_vma=False
    )
```

```python
import functools

import jax
import jax.numpy as jnp
from jax import lax
from jax.experimental import pallas as pl
from jax.experimental.pallas import tpu as pltpu
from jax.sharding import PartitionSpec as P

F32 = jnp.float32
BF16 = jnp.bfloat16
BOTH = ("corpus", "query")
NT = (((1,), (1,)), ((), ()))
TN = (((0,), (0,)), ((), ()))
MIB = 1 << 20
LIVE = 81920.0


def exchange(array, corpus_bits, query_bits):
    pairs = [
        (c * 8 + q, (c ^ corpus_bits) * 8 + (q ^ query_bits))
        for c in range(32)
        for q in range(8)
    ]
    return lax.ppermute(array, BOTH, pairs)


def along_z(array, partner):
    pairs = []
    for c in range(32):
        for q in range(8):
            z = partner[(q >> 2) * 4 + (c >> 3)]
            pairs.append((c * 8 + q, ((z & 3) * 8 + (c & 7)) * 8 + (z >> 2) * 4 + (q & 3)))
    return lax.ppermute(array, BOTH, pairs)


def sides_kernel(lengths_ref, inputs_ref, cotangents_ref, maps_ref, queries_ref, sides_ref, passed_ref,
                 read_in, read_out, maps, sem):
    rank = maps_ref.shape[1] // 2
    sequences = lengths_ref.shape[0]
    slots = inputs_ref.shape[0] // sequences
    first = pltpu.make_async_copy(maps_ref, maps, sem.at[2 * sequences])
    first.start()
    copies = []
    for s in range(sequences):
        rows = pl.ds(s * slots, slots)
        copies.append(pltpu.make_async_copy(inputs_ref.at[rows], read_in.at[rows], sem.at[2 * s]))
        copies.append(pltpu.make_async_copy(cotangents_ref.at[rows], read_out.at[rows], sem.at[2 * s + 1]))
    for copy in copies:
        copy.start()
    last = pltpu.make_async_copy(queries_ref, passed_ref, sem.at[2 * sequences + 1])
    last.start()
    first.wait()
    row = lax.broadcasted_iota(jnp.int32, (slots, 2 * rank), 0)
    lane = lax.broadcasted_iota(jnp.int32, (slots, 2 * rank), 1)
    for s in range(sequences):
        rows = pl.ds(s * slots, slots)
        copies[2 * s].wait()
        of_in = jnp.dot(read_in[rows], maps[...], preferred_element_type=F32)
        copies[2 * s + 1].wait()
        of_out = jnp.dot(read_out[rows], maps[...], preferred_element_type=F32)
        sides = jnp.where(row < lengths_ref[s], jnp.where(lane < rank, of_in, of_out), 0.0)
        sides_ref[rows] = sides.astype(BF16)
    last.wait()


def sides_of(inputs, cotangents, sketch_maps, lengths, queries):
    rows, width = inputs.shape
    both = sketch_maps.shape[1]
    sequences = lengths.shape[0]
    anywhere = pl.BlockSpec(memory_space=pl.ANY)
    return pl.pallas_call(
        sides_kernel,
        in_specs=[pl.BlockSpec(memory_space=pltpu.SMEM)] + [anywhere] * 4,
        out_specs=[pl.BlockSpec(memory_space=pltpu.VMEM)] * 2,
        scratch_shapes=[
            pltpu.VMEM((rows, width), BF16),
            pltpu.VMEM((rows, width), BF16),
            pltpu.VMEM((width, both), BF16),
            pltpu.SemaphoreType.DMA((2 * sequences + 2,)),
        ],
        out_shape=[
            jax.ShapeDtypeStruct((rows, both), BF16),
            jax.ShapeDtypeStruct(queries.shape, BF16),
        ],
        compiler_params=pltpu.CompilerParams(vmem_limit_bytes=56 * MIB),
        cost_estimate=pl.CostEstimate(
            flops=4 * rows * width * both, bytes_accessed=4 * rows * width, transcendentals=0
        ),
    )(lengths, inputs, cotangents, sketch_maps, queries)


def moments_kernel(*refs):
    *parts, out_ref = refs
    rank = out_ref.shape[0]
    total = jnp.zeros((2 * rank, 2 * rank), F32)
    for part in parts:
        total += lax.dot_general(part[...], part[...], TN, preferred_element_type=F32)
    lane = lax.broadcasted_iota(jnp.int32, out_ref.shape, 1)
    out_ref[...] = jnp.where(lane < rank, total[:rank], total[rank:])


def moments_of(parts):
    both = parts[0].shape[1]
    vmem = pl.BlockSpec(memory_space=pltpu.VMEM)
    return pl.pallas_call(
        moments_kernel,
        in_specs=[vmem] * len(parts),
        out_specs=vmem,
        out_shape=jax.ShapeDtypeStruct((both // 2, both), F32),
        compiler_params=pltpu.CompilerParams(vmem_limit_bytes=16 * MIB),
    )(*parts)


def damped_inverses(sums):
    rank = sums.shape[0]
    shape = (rank, 2 * rank)
    row = lax.broadcasted_iota(jnp.int32, shape, 0)
    lane = lax.broadcasted_iota(jnp.int32, shape, 1)
    left = lane < rank
    column = jnp.where(left, lane, lane - rank)
    moment = sums / LIVE
    diagonal = jnp.where(row == column, moment, 0.0)
    trace_in = jnp.sum(jnp.where(left, diagonal, 0.0))
    trace_out = jnp.sum(jnp.where(left, 0.0, diagonal))
    damping = 0.1 / rank * jnp.where(left, trace_in, trace_out)
    work = moment + jnp.where(row == column, damping, 0.0)
    size = 8
    within = lax.broadcasted_iota(jnp.int32, (size, 2 * rank), 0)
    for first in range(0, rank, size):
        wide = [
            jnp.where(left, work[:, k : k + 1], work[:, rank + k : rank + k + 1])
            for k in range(first, first + size)
        ]
        offset = column - first
        inside = (offset >= 0) & (offset < size)
        pivots = [w[first : first + size] for w in wide]
        rows = jnp.where(inside[:size], jnp.where(offset[:size] == within, 1.0, 0.0), work[first : first + size])
        for k in range(size):
            inverse = reciprocal(pivots[k][k : k + 1])
            factor = jnp.where(within == k, 0.0, pivots[k])
            own = rows[k : k + 1] * inverse
            rows = jnp.where(within == k, own, rows - factor * own)
            for later in range(k + 1, size):
                own = pivots[later][k : k + 1] * inverse
                pivots[later] = jnp.where(within == k, own, pivots[later] - factor * own)
        rest = jnp.where(inside, 0.0, work)
        for k in range(size):
            rest = rest - wide[k] * rows[k : k + 1]
        work = jnp.concatenate(
            [rows if k == first else rest[k : k + size] for k in range(0, rank, size)]
        )
    return work


def reciprocal(value):
    guess = pl.reciprocal(value, approx=True)
    guess = guess * (2.0 - value * guess)
    return guess * (2.0 - value * guess)


def scores_kernel(place_ref, sums_ref, near_ref, far_ref, *rest, tile, together):
    *parts, out_ref, held, blocks, sketches, lhs, turned, moved, ready, in_sem, out_sem = rest
    rank = sums_ref.shape[0]
    near = near_ref.shape[0]
    part = parts[0].shape[0]
    tiles = blocks.shape[0] // tile
    rounds = tiles // together

    def build(index, into):
        own = turned.at[index]
        of_in = own[:rank, :]
        for i in range(rank):
            into[i * rank : (i + 1) * rank, :] = (own[rank + i : rank + i + 1, :] * of_in).astype(BF16)

    def score(sketch, moved):
        product = jnp.dot(held[...], sketch[...], preferred_element_type=F32)
        for slot in range(product.shape[0] // 8):
            difference = (slot & 3) * 8 + ((slot >> 2) & 3) * 2 + (slot >> 4)
            target = pl.multiple_of((place_ref[0] ^ difference) * 8, 8)
            moved[pl.ds(target, 8), :] = product[slot * 8 : (slot + 1) * 8, :]
        return moved[...].T

    copies = [
        pltpu.make_async_copy(near_ref, held.at[pl.ds(0, near), :], in_sem.at[0]),
        pltpu.make_async_copy(far_ref, held.at[pl.ds(near, near), :], in_sem.at[1]),
    ]
    for i, ref in enumerate(parts):
        copies.append(pltpu.make_async_copy(ref, blocks.at[pl.ds(i * part, part), :], in_sem.at[2 + i]))
    for copy in copies:
        copy.start()
    inverses = damped_inverses(sums_ref[...])
    left = lax.broadcasted_iota(jnp.int32, inverses.shape, 1) < rank
    whole = jnp.concatenate([jnp.where(left, inverses, 0.0), jnp.where(left, 0.0, inverses)])
    high = whole.astype(BF16)
    lhs[: 2 * rank, :] = high
    lhs[2 * rank :, :] = (whole - high.astype(F32)).astype(BF16)
    for copy in copies:
        copy.wait()
    for index in range(tiles):
        sides = blocks[index * tile : (index + 1) * tile, :]
        both = lax.dot_general(lhs[...], sides, NT, preferred_element_type=F32)
        turned[index] = both[: 2 * rank] + both[2 * rank :]
    build(0, sketches[0])

    def written(round_, h):
        index = round_ * together + h
        slot = index // (part // 2 // tile)
        block = place_ref[1] ^ ((slot & 1) * 4 + (slot >> 1))
        row = block * (part // 2) + (index % (part // 2 // tile)) * tile
        buffer = (round_ % 2) * together + h
        return pltpu.make_async_copy(
            ready.at[buffer], out_ref.at[pl.ds(pl.multiple_of(row, tile), tile), :], out_sem.at[buffer]
        )

    @pl.loop(0, rounds)
    def _(round_):
        @pl.when(round_ >= 2)
        def _():
            for h in range(together):
                written(round_ - 2, h).wait()

        for h in range(together):
            ready[(round_ % 2) * together + h] = score(sketches[h % 2], moved[h % 2])
            build(jnp.minimum(round_ * together + h + 1, tiles - 1), sketches[(h + 1) % 2])
        for h in range(together):
            written(round_, h).start()

    for round_ in (rounds - 2, rounds - 1):
        for h in range(together):
            written(round_, h).wait()


def scores_of(place, sums, near, far, parts, tile=256, together=4):
    both = sums.shape[1]
    number, entries = 2 * near.shape[0], near.shape[1]
    rows = sum(part.shape[0] for part in parts)
    anywhere = pl.BlockSpec(memory_space=pl.ANY)
    return pl.pallas_call(
        functools.partial(scores_kernel, tile=tile, together=together),
        in_specs=[pl.BlockSpec(memory_space=pltpu.SMEM), pl.BlockSpec(memory_space=pltpu.VMEM)]
        + [anywhere] * (2 + len(parts)),
        out_specs=anywhere,
        scratch_shapes=[
            pltpu.VMEM((number, entries), BF16),
            pltpu.VMEM((rows, both), BF16),
            [pltpu.VMEM((entries, tile), BF16)] * 2,
            pltpu.VMEM((2 * both, both), BF16),
            pltpu.VMEM((rows // tile, both, tile), F32),
            [pltpu.VMEM((number, tile), F32)] * 2,
            pltpu.VMEM((2 * together, tile, number), F32),
            pltpu.SemaphoreType.DMA((2 + len(parts),)),
            pltpu.SemaphoreType.DMA((2 * together,)),
        ],
        out_shape=jax.ShapeDtypeStruct((rows, number), F32),
        compiler_params=pltpu.CompilerParams(vmem_limit_bytes=32 * MIB),
        cost_estimate=pl.CostEstimate(
            flops=2 * rows * number * entries, bytes_accessed=4 * rows * number, transcendentals=0
        ),
    )(place, sums, near, far, *parts)


def shards(inputs, cotangents, sketch_maps, lengths, queries):
    sides, queries = sides_of(inputs, cotangents, sketch_maps, lengths, queries)
    pair = jnp.concatenate([sides, exchange(sides, 0, 4)])
    line = jnp.concatenate([queries] + [exchange(queries, 8 * d, 0) for d in (1, 2, 3)])
    pair, line = lax.optimization_barrier((pair, line))
    parts = [pair] + [exchange(pair, 0, d) for d in (1, 2, 3)]
    lines = [line] + [exchange(line, 2 * d, 0) for d in (1, 2, 3)]
    sums = moments_of(parts)
    for d in (1, 8, 16):
        sums = sums + exchange(sums, d, 0)
    *lines, sums = lax.optimization_barrier((*lines, sums))
    sums = sums + (exchange(sums, 2, 0) + exchange(sums, 4, 0) + exchange(sums, 6, 0))
    near = jnp.concatenate(lines)
    far = exchange(near, 1, 0)
    place = jnp.stack([lax.axis_index("corpus"), lax.axis_index("query")]).astype(jnp.int32)
    return scores_of(place, sums, near, far, parts)


def solution(mesh):
    placed = (
        P(BOTH, None),
        P(BOTH, None),
        P(),
        P(BOTH),
        P(("query", "corpus"), None),
    )
    return jax.shard_map(
        shards, mesh=mesh, in_specs=placed, out_specs=P("corpus", "query"), check_vma=False
    )
```

```python
import functools

import jax
import jax.numpy as jnp
from jax import lax
from jax.experimental import pallas as pl
from jax.experimental.pallas import tpu as pltpu
from jax.sharding import PartitionSpec as P

F32 = jnp.float32
BF16 = jnp.bfloat16
BOTH = ("corpus", "query")
NT = (((1,), (1,)), ((), ()))
TN = (((0,), (0,)), ((), ()))
MIB = 1 << 20
LIVE = 81920.0


def exchange(array, corpus_bits, query_bits):
    pairs = [
        (c * 8 + q, (c ^ corpus_bits) * 8 + (q ^ query_bits))
        for c in range(32)
        for q in range(8)
    ]
    return lax.ppermute(array, BOTH, pairs)


def along_z(array, partner):
    pairs = []
    for c in range(32):
        for q in range(8):
            z = partner[(q >> 2) * 4 + (c >> 3)]
            pairs.append((c * 8 + q, ((z & 3) * 8 + (c & 7)) * 8 + (z >> 2) * 4 + (q & 3)))
    return lax.ppermute(array, BOTH, pairs)


def sides_kernel(lengths_ref, inputs_ref, cotangents_ref, maps_ref, sides_ref, read_in, read_out, maps, sem):
    rank = maps_ref.shape[1] // 2
    sequences = lengths_ref.shape[0]
    slots = inputs_ref.shape[0] // sequences
    first = pltpu.make_async_copy(maps_ref, maps, sem.at[2 * sequences])
    first.start()
    copies = []
    for s in range(sequences):
        rows = pl.ds(s * slots, slots)
        copies.append(pltpu.make_async_copy(inputs_ref.at[rows], read_in.at[rows], sem.at[2 * s]))
        copies.append(pltpu.make_async_copy(cotangents_ref.at[rows], read_out.at[rows], sem.at[2 * s + 1]))
    for copy in copies:
        copy.start()
    first.wait()
    row = lax.broadcasted_iota(jnp.int32, (slots, 2 * rank), 0)
    lane = lax.broadcasted_iota(jnp.int32, (slots, 2 * rank), 1)
    for s in range(sequences):
        rows = pl.ds(s * slots, slots)
        copies[2 * s].wait()
        of_in = jnp.dot(read_in[rows], maps[...], preferred_element_type=F32)
        copies[2 * s + 1].wait()
        of_out = jnp.dot(read_out[rows], maps[...], preferred_element_type=F32)
        sides = jnp.where(row < lengths_ref[s], jnp.where(lane < rank, of_in, of_out), 0.0)
        sides_ref[rows] = sides.astype(BF16)


def sides_of(inputs, cotangents, sketch_maps, lengths):
    rows, width = inputs.shape
    both = sketch_maps.shape[1]
    sequences = lengths.shape[0]
    anywhere = pl.BlockSpec(memory_space=pl.ANY)
    return pl.pallas_call(
        sides_kernel,
        in_specs=[pl.BlockSpec(memory_space=pltpu.SMEM)] + [anywhere] * 3,
        out_specs=pl.BlockSpec(memory_space=pltpu.VMEM),
        scratch_shapes=[
            pltpu.VMEM((rows, width), BF16),
            pltpu.VMEM((rows, width), BF16),
            pltpu.VMEM((width, both), BF16),
            pltpu.SemaphoreType.DMA((2 * sequences + 1,)),
        ],
        out_shape=jax.ShapeDtypeStruct((rows, both), BF16),
        compiler_params=pltpu.CompilerParams(vmem_limit_bytes=56 * MIB),
        cost_estimate=pl.CostEstimate(
            flops=4 * rows * width * both, bytes_accessed=4 * rows * width, transcendentals=0
        ),
    )(lengths, inputs, cotangents, sketch_maps)


def moments_kernel(*refs):
    *parts, out_ref = refs
    rank = out_ref.shape[0]
    total = jnp.zeros((2 * rank, 2 * rank), F32)
    for part in parts:
        total += lax.dot_general(part[...], part[...], TN, preferred_element_type=F32)
    lane = lax.broadcasted_iota(jnp.int32, out_ref.shape, 1)
    out_ref[...] = jnp.where(lane < rank, total[:rank], total[rank:])


def moments_of(parts):
    both = parts[0].shape[1]
    vmem = pl.BlockSpec(memory_space=pltpu.VMEM)
    return pl.pallas_call(
        moments_kernel,
        in_specs=[vmem] * len(parts),
        out_specs=vmem,
        out_shape=jax.ShapeDtypeStruct((both // 2, both), F32),
        compiler_params=pltpu.CompilerParams(vmem_limit_bytes=16 * MIB),
    )(*parts)


def damped_inverses(sums):
    rank = sums.shape[0]
    shape = (rank, 2 * rank)
    row = lax.broadcasted_iota(jnp.int32, shape, 0)
    lane = lax.broadcasted_iota(jnp.int32, shape, 1)
    left = lane < rank
    column = jnp.where(left, lane, lane - rank)
    moment = sums / LIVE
    diagonal = jnp.where(row == column, moment, 0.0)
    trace_in = jnp.sum(jnp.where(left, diagonal, 0.0))
    trace_out = jnp.sum(jnp.where(left, 0.0, diagonal))
    damping = 0.1 / rank * jnp.where(left, trace_in, trace_out)
    work = moment + jnp.where(row == column, damping, 0.0)
    size = 8
    within = lax.broadcasted_iota(jnp.int32, (size, 2 * rank), 0)
    for first in range(0, rank, size):
        wide = [
            jnp.where(left, work[:, k : k + 1], work[:, rank + k : rank + k + 1])
            for k in range(first, first + size)
        ]
        offset = column - first
        inside = (offset >= 0) & (offset < size)
        pivots = [w[first : first + size] for w in wide]
        rows = jnp.where(inside[:size], jnp.where(offset[:size] == within, 1.0, 0.0), work[first : first + size])
        for k in range(size):
            inverse = reciprocal(pivots[k][k : k + 1])
            factor = jnp.where(within == k, 0.0, pivots[k])
            own = rows[k : k + 1] * inverse
            rows = jnp.where(within == k, own, rows - factor * own)
            for later in range(k + 1, size):
                own = pivots[later][k : k + 1] * inverse
                pivots[later] = jnp.where(within == k, own, pivots[later] - factor * own)
        rest = jnp.where(inside, 0.0, work)
        for k in range(size):
            rest = rest - wide[k] * rows[k : k + 1]
        work = jnp.concatenate(
            [rows if k == first else rest[k : k + size] for k in range(0, rank, size)]
        )
    return work


def reciprocal(value):
    guess = pl.reciprocal(value, approx=True)
    guess = guess * (2.0 - value * guess)
    return guess * (2.0 - value * guess)


def scores_kernel(place_ref, sums_ref, near_ref, far_ref, *rest, tile, together):
    *parts, out_ref, held, blocks, sketches, lhs, turned, moved, ready, in_sem, out_sem = rest
    rank = sums_ref.shape[0]
    near = near_ref.shape[0]
    part = parts[0].shape[0]
    tiles = blocks.shape[0] // tile
    rounds = tiles // together

    def build(index, into):
        own = turned.at[index]
        of_in = own[:rank, :]
        for i in range(rank):
            into[i * rank : (i + 1) * rank, :] = (own[rank + i : rank + i + 1, :] * of_in).astype(BF16)

    def score(sketch, moved):
        product = jnp.dot(held[...], sketch[...], preferred_element_type=F32)
        for slot in range(product.shape[0] // 8):
            difference = (slot & 3) * 8 + ((slot >> 2) & 3) * 2 + (slot >> 4)
            target = pl.multiple_of((place_ref[0] ^ difference) * 8, 8)
            moved[pl.ds(target, 8), :] = product[slot * 8 : (slot + 1) * 8, :]
        return moved[...].T

    copies = [
        pltpu.make_async_copy(near_ref, held.at[pl.ds(0, near), :], in_sem.at[0]),
        pltpu.make_async_copy(far_ref, held.at[pl.ds(near, near), :], in_sem.at[1]),
    ]
    for i, ref in enumerate(parts):
        copies.append(pltpu.make_async_copy(ref, blocks.at[pl.ds(i * part, part), :], in_sem.at[2 + i]))
    for copy in copies:
        copy.start()
    inverses = damped_inverses(sums_ref[...])
    left = lax.broadcasted_iota(jnp.int32, inverses.shape, 1) < rank
    whole = jnp.concatenate([jnp.where(left, inverses, 0.0), jnp.where(left, 0.0, inverses)])
    high = whole.astype(BF16)
    lhs[: 2 * rank, :] = high
    lhs[2 * rank :, :] = (whole - high.astype(F32)).astype(BF16)
    for copy in copies:
        copy.wait()
    for index in range(tiles):
        sides = blocks[index * tile : (index + 1) * tile, :]
        both = lax.dot_general(lhs[...], sides, NT, preferred_element_type=F32)
        turned[index] = both[: 2 * rank] + both[2 * rank :]
    build(0, sketches[0])

    def written(round_, h):
        index = round_ * together + h
        slot = index // (part // 2 // tile)
        block = place_ref[1] ^ ((slot & 1) * 4 + (slot >> 1))
        row = block * (part // 2) + (index % (part // 2 // tile)) * tile
        buffer = (round_ % 2) * together + h
        return pltpu.make_async_copy(
            ready.at[buffer], out_ref.at[pl.ds(pl.multiple_of(row, tile), tile), :], out_sem.at[buffer]
        )

    @pl.loop(0, rounds)
    def _(round_):
        @pl.when(round_ >= 2)
        def _():
            for h in range(together):
                written(round_ - 2, h).wait()

        for h in range(together):
            ready[(round_ % 2) * together + h] = score(sketches[h % 2], moved[h % 2])
            build(jnp.minimum(round_ * together + h + 1, tiles - 1), sketches[(h + 1) % 2])
        for h in range(together):
            written(round_, h).start()

    for round_ in (rounds - 2, rounds - 1):
        for h in range(together):
            written(round_, h).wait()


def scores_of(place, sums, near, far, parts, tile=256, together=4):
    both = sums.shape[1]
    number, entries = 2 * near.shape[0], near.shape[1]
    rows = sum(part.shape[0] for part in parts)
    anywhere = pl.BlockSpec(memory_space=pl.ANY)
    return pl.pallas_call(
        functools.partial(scores_kernel, tile=tile, together=together),
        in_specs=[pl.BlockSpec(memory_space=pltpu.SMEM), pl.BlockSpec(memory_space=pltpu.VMEM)]
        + [anywhere] * (2 + len(parts)),
        out_specs=anywhere,
        scratch_shapes=[
            pltpu.VMEM((number, entries), BF16),
            pltpu.VMEM((rows, both), BF16),
            [pltpu.VMEM((entries, tile), BF16)] * 2,
            pltpu.VMEM((2 * both, both), BF16),
            pltpu.VMEM((rows // tile, both, tile), F32),
            [pltpu.VMEM((number, tile), F32)] * 2,
            pltpu.VMEM((2 * together, tile, number), F32),
            pltpu.SemaphoreType.DMA((2 + len(parts),)),
            pltpu.SemaphoreType.DMA((2 * together,)),
        ],
        out_shape=jax.ShapeDtypeStruct((rows, number), F32),
        compiler_params=pltpu.CompilerParams(vmem_limit_bytes=32 * MIB),
        cost_estimate=pl.CostEstimate(
            flops=2 * rows * number * entries, bytes_accessed=4 * rows * number, transcendentals=0
        ),
    )(place, sums, near, far, *parts)


def shards(inputs, cotangents, sketch_maps, lengths, queries):
    line = jnp.concatenate([queries] + [exchange(queries, 8 * d, 0) for d in (1, 2, 3)])
    sides = sides_of(inputs, cotangents, sketch_maps, lengths)
    sides, line = lax.optimization_barrier((sides, line))
    pair = jnp.concatenate([sides, exchange(sides, 0, 4)])
    parts = [pair] + [exchange(pair, 0, d) for d in (1, 2, 3)]
    lines = [line] + [exchange(line, 2 * d, 0) for d in (1, 2, 3)]
    sums = moments_of(parts)
    for d in (1, 8, 16):
        sums = sums + exchange(sums, d, 0)
    *lines, sums = lax.optimization_barrier((*lines, sums))
    sums = sums + (exchange(sums, 2, 0) + exchange(sums, 4, 0) + exchange(sums, 6, 0))
    near = jnp.concatenate(lines)
    far = exchange(near, 1, 0)
    place = jnp.stack([lax.axis_index("corpus"), lax.axis_index("query")]).astype(jnp.int32)
    return scores_of(place, sums, near, far, parts)


def solution(mesh):
    placed = (
        P(BOTH, None),
        P(BOTH, None),
        P(),
        P(BOTH),
        P(("query", "corpus"), None),
    )
    return jax.shard_map(
        shards, mesh=mesh, in_specs=placed, out_specs=P("corpus", "query"), check_vma=False
    )
```

```python
import functools

import jax
import jax.numpy as jnp
from jax import lax
from jax.experimental import pallas as pl
from jax.experimental.pallas import tpu as pltpu
from jax.sharding import PartitionSpec as P

F32 = jnp.float32
BF16 = jnp.bfloat16
BOTH = ("corpus", "query")
NT = (((1,), (1,)), ((), ()))
TN = (((0,), (0,)), ((), ()))
MIB = 1 << 20
LIVE = 81920.0


def exchange(array, corpus_bits, query_bits):
    pairs = [
        (c * 8 + q, (c ^ corpus_bits) * 8 + (q ^ query_bits))
        for c in range(32)
        for q in range(8)
    ]
    return lax.ppermute(array, BOTH, pairs)


def along_z(array, partner):
    pairs = []
    for c in range(32):
        for q in range(8):
            z = partner[(q >> 2) * 4 + (c >> 3)]
            pairs.append((c * 8 + q, ((z & 3) * 8 + (c & 7)) * 8 + (z >> 2) * 4 + (q & 3)))
    return lax.ppermute(array, BOTH, pairs)


def sides_kernel(lengths_ref, inputs_ref, cotangents_ref, maps_ref, sides_ref, read_in, read_out, maps, sem, ahead=3):
    rank = maps_ref.shape[1] // 2
    sequences = lengths_ref.shape[0]
    slots = inputs_ref.shape[0] // sequences
    first = pltpu.make_async_copy(maps_ref, maps, sem.at[2 * sequences])
    first.start()
    copies = []
    for s in range(sequences):
        rows = pl.ds(s * slots, slots)
        copies.append(pltpu.make_async_copy(inputs_ref.at[rows], read_in.at[rows], sem.at[2 * s]))
        copies.append(pltpu.make_async_copy(cotangents_ref.at[rows], read_out.at[rows], sem.at[2 * s + 1]))
    for copy in copies[: 2 * ahead]:
        copy.start()
    first.wait()
    row = lax.broadcasted_iota(jnp.int32, (slots, 2 * rank), 0)
    lane = lax.broadcasted_iota(jnp.int32, (slots, 2 * rank), 1)
    for s in range(sequences):
        rows = pl.ds(s * slots, slots)
        copies[2 * s].wait()
        copies[2 * s + 1].wait()
        for copy in copies[2 * (s + ahead) : 2 * (s + ahead + 1)]:
            copy.start()
        of_in = jnp.dot(read_in[rows], maps[...], preferred_element_type=F32)
        of_out = jnp.dot(read_out[rows], maps[...], preferred_element_type=F32)
        sides = jnp.where(row < lengths_ref[s], jnp.where(lane < rank, of_in, of_out), 0.0)
        sides_ref[rows] = sides.astype(BF16)


def sides_of(inputs, cotangents, sketch_maps, lengths):
    rows, width = inputs.shape
    both = sketch_maps.shape[1]
    sequences = lengths.shape[0]
    anywhere = pl.BlockSpec(memory_space=pl.ANY)
    return pl.pallas_call(
        sides_kernel,
        in_specs=[pl.BlockSpec(memory_space=pltpu.SMEM)] + [anywhere] * 3,
        out_specs=pl.BlockSpec(memory_space=pltpu.VMEM),
        scratch_shapes=[
            pltpu.VMEM((rows, width), BF16),
            pltpu.VMEM((rows, width), BF16),
            pltpu.VMEM((width, both), BF16),
            pltpu.SemaphoreType.DMA((2 * sequences + 1,)),
        ],
        out_shape=jax.ShapeDtypeStruct((rows, both), BF16),
        compiler_params=pltpu.CompilerParams(vmem_limit_bytes=56 * MIB),
        cost_estimate=pl.CostEstimate(
            flops=4 * rows * width * both, bytes_accessed=4 * rows * width, transcendentals=0
        ),
    )(lengths, inputs, cotangents, sketch_maps)


def moments_kernel(*refs):
    *parts, out_ref = refs
    rank = out_ref.shape[0]
    total = jnp.zeros((2 * rank, 2 * rank), F32)
    for part in parts:
        total += lax.dot_general(part[...], part[...], TN, preferred_element_type=F32)
    lane = lax.broadcasted_iota(jnp.int32, out_ref.shape, 1)
    out_ref[...] = jnp.where(lane < rank, total[:rank], total[rank:])


def moments_of(parts):
    both = parts[0].shape[1]
    vmem = pl.BlockSpec(memory_space=pltpu.VMEM)
    return pl.pallas_call(
        moments_kernel,
        in_specs=[vmem] * len(parts),
        out_specs=vmem,
        out_shape=jax.ShapeDtypeStruct((both // 2, both), F32),
        compiler_params=pltpu.CompilerParams(vmem_limit_bytes=16 * MIB),
    )(*parts)


def damped_inverses(sums):
    rank = sums.shape[0]
    shape = (rank, 2 * rank)
    row = lax.broadcasted_iota(jnp.int32, shape, 0)
    lane = lax.broadcasted_iota(jnp.int32, shape, 1)
    left = lane < rank
    column = jnp.where(left, lane, lane - rank)
    moment = sums / LIVE
    diagonal = jnp.where(row == column, moment, 0.0)
    trace_in = jnp.sum(jnp.where(left, diagonal, 0.0))
    trace_out = jnp.sum(jnp.where(left, 0.0, diagonal))
    damping = 0.1 / rank * jnp.where(left, trace_in, trace_out)
    work = moment + jnp.where(row == column, damping, 0.0)
    size = 8
    within = lax.broadcasted_iota(jnp.int32, (size, 2 * rank), 0)
    for first in range(0, rank, size):
        wide = [
            jnp.where(left, work[:, k : k + 1], work[:, rank + k : rank + k + 1])
            for k in range(first, first + size)
        ]
        offset = column - first
        inside = (offset >= 0) & (offset < size)
        pivots = [w[first : first + size] for w in wide]
        rows = jnp.where(inside[:size], jnp.where(offset[:size] == within, 1.0, 0.0), work[first : first + size])
        for k in range(size):
            inverse = reciprocal(pivots[k][k : k + 1])
            factor = jnp.where(within == k, 0.0, pivots[k])
            own = rows[k : k + 1] * inverse
            rows = jnp.where(within == k, own, rows - factor * own)
            for later in range(k + 1, size):
                own = pivots[later][k : k + 1] * inverse
                pivots[later] = jnp.where(within == k, own, pivots[later] - factor * own)
        rest = jnp.where(inside, 0.0, work)
        for k in range(size):
            rest = rest - wide[k] * rows[k : k + 1]
        work = jnp.concatenate(
            [rows if k == first else rest[k : k + size] for k in range(0, rank, size)]
        )
    return work


def reciprocal(value):
    guess = pl.reciprocal(value, approx=True)
    guess = guess * (2.0 - value * guess)
    return guess * (2.0 - value * guess)


def scores_kernel(place_ref, sums_ref, near_ref, far_ref, *rest, tile, together):
    *parts, out_ref, held, blocks, sketches, lhs, turned, moved, ready, in_sem, out_sem = rest
    rank = sums_ref.shape[0]
    near = near_ref.shape[0]
    part = parts[0].shape[0]
    tiles = blocks.shape[0] // tile
    rounds = tiles // together

    def build(index, into):
        own = turned.at[index]
        of_in = own[:rank, :]
        for i in range(rank):
            into[i * rank : (i + 1) * rank, :] = (own[rank + i : rank + i + 1, :] * of_in).astype(BF16)

    def score(sketch, moved):
        product = jnp.dot(held[...], sketch[...], preferred_element_type=F32)
        for slot in range(product.shape[0] // 8):
            difference = (slot & 3) * 8 + ((slot >> 2) & 3) * 2 + (slot >> 4)
            target = pl.multiple_of((place_ref[0] ^ difference) * 8, 8)
            moved[pl.ds(target, 8), :] = product[slot * 8 : (slot + 1) * 8, :]
        return moved[...].T

    copies = [
        pltpu.make_async_copy(near_ref, held.at[pl.ds(0, near), :], in_sem.at[0]),
        pltpu.make_async_copy(far_ref, held.at[pl.ds(near, near), :], in_sem.at[1]),
    ]
    for i, ref in enumerate(parts):
        copies.append(pltpu.make_async_copy(ref, blocks.at[pl.ds(i * part, part), :], in_sem.at[2 + i]))
    for copy in copies:
        copy.start()
    inverses = damped_inverses(sums_ref[...])
    left = lax.broadcasted_iota(jnp.int32, inverses.shape, 1) < rank
    whole = jnp.concatenate([jnp.where(left, inverses, 0.0), jnp.where(left, 0.0, inverses)])
    high = whole.astype(BF16)
    lhs[: 2 * rank, :] = high
    lhs[2 * rank :, :] = (whole - high.astype(F32)).astype(BF16)
    for copy in copies:
        copy.wait()
    for index in range(tiles):
        sides = blocks[index * tile : (index + 1) * tile, :]
        both = lax.dot_general(lhs[...], sides, NT, preferred_element_type=F32)
        turned[index] = both[: 2 * rank] + both[2 * rank :]
    build(0, sketches[0])

    def written(round_, h):
        index = round_ * together + h
        slot = index // (part // 2 // tile)
        block = place_ref[1] ^ ((slot & 1) * 4 + (slot >> 1))
        row = block * (part // 2) + (index % (part // 2 // tile)) * tile
        buffer = (round_ % 2) * together + h
        return pltpu.make_async_copy(
            ready.at[buffer], out_ref.at[pl.ds(pl.multiple_of(row, tile), tile), :], out_sem.at[buffer]
        )

    @pl.loop(0, rounds)
    def _(round_):
        @pl.when(round_ >= 2)
        def _():
            for h in range(together):
                written(round_ - 2, h).wait()

        for h in range(together):
            build(jnp.minimum(round_ * together + h + 1, tiles - 1), sketches[(h + 1) % 2])
            ready[(round_ % 2) * together + h] = score(sketches[h % 2], moved[h % 2])
            written(round_, h).start()

    for round_ in (rounds - 2, rounds - 1):
        for h in range(together):
            written(round_, h).wait()


def scores_of(place, sums, near, far, parts, tile=256, together=4):
    both = sums.shape[1]
    number, entries = 2 * near.shape[0], near.shape[1]
    rows = sum(part.shape[0] for part in parts)
    anywhere = pl.BlockSpec(memory_space=pl.ANY)
    return pl.pallas_call(
        functools.partial(scores_kernel, tile=tile, together=together),
        in_specs=[pl.BlockSpec(memory_space=pltpu.SMEM), pl.BlockSpec(memory_space=pltpu.VMEM)]
        + [anywhere] * (2 + len(parts)),
        out_specs=anywhere,
        scratch_shapes=[
            pltpu.VMEM((number, entries), BF16),
            pltpu.VMEM((rows, both), BF16),
            [pltpu.VMEM((entries, tile), BF16)] * 2,
            pltpu.VMEM((2 * both, both), BF16),
            pltpu.VMEM((rows // tile, both, tile), F32),
            [pltpu.VMEM((number, tile), F32)] * 2,
            pltpu.VMEM((2 * together, tile, number), F32),
            pltpu.SemaphoreType.DMA((2 + len(parts),)),
            pltpu.SemaphoreType.DMA((2 * together,)),
        ],
        out_shape=jax.ShapeDtypeStruct((rows, number), F32),
        compiler_params=pltpu.CompilerParams(vmem_limit_bytes=32 * MIB),
        cost_estimate=pl.CostEstimate(
            flops=2 * rows * number * entries, bytes_accessed=4 * rows * number, transcendentals=0
        ),
    )(place, sums, near, far, *parts)


def shards(inputs, cotangents, sketch_maps, lengths, queries):
    line = jnp.concatenate([queries] + [exchange(queries, 8 * d, 0) for d in (1, 2, 3)])
    sides = sides_of(inputs, cotangents, sketch_maps, lengths)
    sides, line = lax.optimization_barrier((sides, line))
    pair = jnp.concatenate([sides, exchange(sides, 0, 4)])
    parts = [pair] + [exchange(pair, 0, d) for d in (1, 2, 3)]
    lines = [line] + [exchange(line, 2 * d, 0) for d in (1, 2, 3)]
    sums = moments_of(parts)
    for d in (1, 8, 16):
        sums = sums + exchange(sums, d, 0)
    *lines, sums = lax.optimization_barrier((*lines, sums))
    sums = sums + (exchange(sums, 2, 0) + exchange(sums, 4, 0) + exchange(sums, 6, 0))
    near = jnp.concatenate(lines)
    far = exchange(near, 1, 0)
    place = jnp.stack([lax.axis_index("corpus"), lax.axis_index("query")]).astype(jnp.int32)
    return scores_of(place, sums, near, far, parts)


def solution(mesh):
    placed = (
        P(BOTH, None),
        P(BOTH, None),
        P(),
        P(BOTH),
        P(("query", "corpus"), None),
    )
    return jax.shard_map(
        shards, mesh=mesh, in_specs=placed, out_specs=P("corpus", "query"), check_vma=False
    )
```

```python
import functools

import jax
import jax.numpy as jnp
from jax import lax
from jax.experimental import pallas as pl
from jax.experimental.pallas import tpu as pltpu
from jax.sharding import PartitionSpec as P

F32 = jnp.float32
BF16 = jnp.bfloat16
BOTH = ("corpus", "query")
NT = (((1,), (1,)), ((), ()))
TN = (((0,), (0,)), ((), ()))
MIB = 1 << 20
LIVE = 81920.0


def exchange(array, corpus_bits, query_bits):
    pairs = [
        (c * 8 + q, (c ^ corpus_bits) * 8 + (q ^ query_bits))
        for c in range(32)
        for q in range(8)
    ]
    return lax.ppermute(array, BOTH, pairs)


def along_z(array, partner):
    pairs = []
    for c in range(32):
        for q in range(8):
            z = partner[(q >> 2) * 4 + (c >> 3)]
            pairs.append((c * 8 + q, ((z & 3) * 8 + (c & 7)) * 8 + (z >> 2) * 4 + (q & 3)))
    return lax.ppermute(array, BOTH, pairs)


def sides_kernel(lengths_ref, inputs_ref, cotangents_ref, maps_ref, sides_ref, read_in, read_out, maps, sem, ahead=3):
    rank = maps_ref.shape[1] // 2
    sequences = lengths_ref.shape[0]
    slots = inputs_ref.shape[0] // sequences
    first = pltpu.make_async_copy(maps_ref, maps, sem.at[2 * sequences])
    first.start()
    copies = []
    for s in range(sequences):
        rows = pl.ds(s * slots, slots)
        copies.append(pltpu.make_async_copy(inputs_ref.at[rows], read_in.at[rows], sem.at[2 * s]))
        copies.append(pltpu.make_async_copy(cotangents_ref.at[rows], read_out.at[rows], sem.at[2 * s + 1]))
    for copy in copies[: 2 * ahead]:
        copy.start()
    first.wait()
    row = lax.broadcasted_iota(jnp.int32, (slots, 2 * rank), 0)
    lane = lax.broadcasted_iota(jnp.int32, (slots, 2 * rank), 1)
    for s in range(sequences):
        rows = pl.ds(s * slots, slots)
        copies[2 * s].wait()
        copies[2 * s + 1].wait()
        for copy in copies[2 * (s + ahead) : 2 * (s + ahead + 1)]:
            copy.start()
        of_in = jnp.dot(read_in[rows], maps[...], preferred_element_type=F32)
        of_out = jnp.dot(read_out[rows], maps[...], preferred_element_type=F32)
        sides = jnp.where(row < lengths_ref[s], jnp.where(lane < rank, of_in, of_out), 0.0)
        sides_ref[rows] = sides.astype(BF16)


def sides_of(inputs, cotangents, sketch_maps, lengths):
    rows, width = inputs.shape
    both = sketch_maps.shape[1]
    sequences = lengths.shape[0]
    anywhere = pl.BlockSpec(memory_space=pl.ANY)
    return pl.pallas_call(
        sides_kernel,
        in_specs=[pl.BlockSpec(memory_space=pltpu.SMEM)] + [anywhere] * 3,
        out_specs=pl.BlockSpec(memory_space=pltpu.VMEM),
        scratch_shapes=[
            pltpu.VMEM((rows, width), BF16),
            pltpu.VMEM((rows, width), BF16),
            pltpu.VMEM((width, both), BF16),
            pltpu.SemaphoreType.DMA((2 * sequences + 1,)),
        ],
        out_shape=jax.ShapeDtypeStruct((rows, both), BF16),
        compiler_params=pltpu.CompilerParams(vmem_limit_bytes=56 * MIB),
        cost_estimate=pl.CostEstimate(
            flops=4 * rows * width * both, bytes_accessed=4 * rows * width, transcendentals=0
        ),
    )(lengths, inputs, cotangents, sketch_maps)


def moments_kernel(*refs):
    *parts, out_ref = refs
    rank = out_ref.shape[0]
    total = jnp.zeros((2 * rank, 2 * rank), F32)
    for part in parts:
        total += lax.dot_general(part[...], part[...], TN, preferred_element_type=F32)
    lane = lax.broadcasted_iota(jnp.int32, out_ref.shape, 1)
    out_ref[...] = jnp.where(lane < rank, total[:rank], total[rank:])


def moments_of(parts):
    both = parts[0].shape[1]
    vmem = pl.BlockSpec(memory_space=pltpu.VMEM)
    return pl.pallas_call(
        moments_kernel,
        in_specs=[vmem] * len(parts),
        out_specs=vmem,
        out_shape=jax.ShapeDtypeStruct((both // 2, both), F32),
        compiler_params=pltpu.CompilerParams(vmem_limit_bytes=16 * MIB),
    )(*parts)


def damped_inverses(sums):
    rank = sums.shape[0]
    shape = (rank, 2 * rank)
    row = lax.broadcasted_iota(jnp.int32, shape, 0)
    lane = lax.broadcasted_iota(jnp.int32, shape, 1)
    left = lane < rank
    column = jnp.where(left, lane, lane - rank)
    moment = sums / LIVE
    diagonal = jnp.where(row == column, moment, 0.0)
    trace_in = jnp.sum(jnp.where(left, diagonal, 0.0))
    trace_out = jnp.sum(jnp.where(left, 0.0, diagonal))
    damping = 0.1 / rank * jnp.where(left, trace_in, trace_out)
    work = moment + jnp.where(row == column, damping, 0.0)
    size = 8
    within = lax.broadcasted_iota(jnp.int32, (size, 2 * rank), 0)
    for first in range(0, rank, size):
        wide = [
            jnp.where(left, work[:, k : k + 1], work[:, rank + k : rank + k + 1])
            for k in range(first, first + size)
        ]
        offset = column - first
        inside = (offset >= 0) & (offset < size)
        pivots = [w[first : first + size] for w in wide]
        rows = jnp.where(inside[:size], jnp.where(offset[:size] == within, 1.0, 0.0), work[first : first + size])
        for k in range(size):
            inverse = reciprocal(pivots[k][k : k + 1])
            factor = jnp.where(within == k, 0.0, pivots[k])
            own = rows[k : k + 1] * inverse
            rows = jnp.where(within == k, own, rows - factor * own)
            for later in range(k + 1, size):
                own = pivots[later][k : k + 1] * inverse
                pivots[later] = jnp.where(within == k, own, pivots[later] - factor * own)
        rest = jnp.where(inside, 0.0, work)
        for k in range(size):
            rest = rest - wide[k] * rows[k : k + 1]
        work = jnp.concatenate(
            [rows if k == first else rest[k : k + size] for k in range(0, rank, size)]
        )
    return work


def reciprocal(value):
    guess = pl.reciprocal(value, approx=True)
    guess = guess * (2.0 - value * guess)
    return guess * (2.0 - value * guess)


def scores_kernel(place_ref, sums_ref, near_ref, far_ref, *rest, tile, together):
    *parts, out_ref, held, blocks, sketches, lhs, turned, moved, ready, in_sem, out_sem = rest
    rank = sums_ref.shape[0]
    near = near_ref.shape[0]
    part = parts[0].shape[0]
    tiles = blocks.shape[0] // tile
    rounds = tiles // together

    def build(index, into):
        own = turned.at[index]
        of_in = own[:rank, :]
        for i in range(rank):
            into[i * rank : (i + 1) * rank, :] = (own[rank + i : rank + i + 1, :] * of_in).astype(BF16)

    def score(sketch, moved):
        product = jnp.dot(held[...], sketch[...], preferred_element_type=F32)
        for slot in range(product.shape[0] // 8):
            difference = (slot & 3) * 8 + ((slot >> 2) & 3) * 2 + (slot >> 4)
            target = pl.multiple_of((place_ref[0] ^ difference) * 8, 8)
            moved[pl.ds(target, 8), :] = product[slot * 8 : (slot + 1) * 8, :]
        return moved[...].T

    copies = [
        pltpu.make_async_copy(near_ref, held.at[pl.ds(0, near), :], in_sem.at[0]),
        pltpu.make_async_copy(far_ref, held.at[pl.ds(near, near), :], in_sem.at[1]),
    ]
    for i, ref in enumerate(parts):
        copies.append(pltpu.make_async_copy(ref, blocks.at[pl.ds(i * part, part), :], in_sem.at[2 + i]))
    for copy in copies:
        copy.start()
    inverses = damped_inverses(sums_ref[...])
    left = lax.broadcasted_iota(jnp.int32, inverses.shape, 1) < rank
    whole = jnp.concatenate([jnp.where(left, inverses, 0.0), jnp.where(left, 0.0, inverses)])
    high = whole.astype(BF16)
    lhs[: 2 * rank, :] = high
    lhs[2 * rank :, :] = (whole - high.astype(F32)).astype(BF16)
    for copy in copies:
        copy.wait()
    for index in range(tiles):
        sides = blocks[index * tile : (index + 1) * tile, :]
        both = lax.dot_general(lhs[...], sides, NT, preferred_element_type=F32)
        turned[index] = both[: 2 * rank] + both[2 * rank :]
    build(0, sketches[0])

    def written(round_, h):
        index = round_ * together + h
        slot = index // (part // 2 // tile)
        block = place_ref[1] ^ ((slot & 1) * 4 + (slot >> 1))
        row = block * (part // 2) + (index % (part // 2 // tile)) * tile
        buffer = (round_ % 2) * together + h
        return pltpu.make_async_copy(
            ready.at[buffer], out_ref.at[pl.ds(pl.multiple_of(row, tile), tile), :], out_sem.at[buffer]
        )

    @pl.loop(0, rounds)
    def _(round_):
        @pl.when(round_ >= 2)
        def _():
            for h in range(together):
                written(round_ - 2, h).wait()

        for h in range(together):
            build(jnp.minimum(round_ * together + h + 1, tiles - 1), sketches[(h + 1) % 2])
            ready[(round_ % 2) * together + h] = score(sketches[h % 2], moved[h % 2])
            written(round_, h).start()

    for round_ in (rounds - 2, rounds - 1):
        for h in range(together):
            written(round_, h).wait()


def scores_of(place, sums, near, far, parts, tile=256, together=8):
    both = sums.shape[1]
    number, entries = 2 * near.shape[0], near.shape[1]
    rows = sum(part.shape[0] for part in parts)
    anywhere = pl.BlockSpec(memory_space=pl.ANY)
    return pl.pallas_call(
        functools.partial(scores_kernel, tile=tile, together=together),
        in_specs=[pl.BlockSpec(memory_space=pltpu.SMEM), pl.BlockSpec(memory_space=pltpu.VMEM)]
        + [anywhere] * (2 + len(parts)),
        out_specs=anywhere,
        scratch_shapes=[
            pltpu.VMEM((number, entries), BF16),
            pltpu.VMEM((rows, both), BF16),
            [pltpu.VMEM((entries, tile), BF16)] * 2,
            pltpu.VMEM((2 * both, both), BF16),
            pltpu.VMEM((rows // tile, both, tile), F32),
            [pltpu.VMEM((number, tile), F32)] * 2,
            pltpu.VMEM((2 * together, tile, number), F32),
            pltpu.SemaphoreType.DMA((2 + len(parts),)),
            pltpu.SemaphoreType.DMA((2 * together,)),
        ],
        out_shape=jax.ShapeDtypeStruct((rows, number), F32),
        compiler_params=pltpu.CompilerParams(vmem_limit_bytes=32 * MIB),
        cost_estimate=pl.CostEstimate(
            flops=2 * rows * number * entries, bytes_accessed=4 * rows * number, transcendentals=0
        ),
    )(place, sums, near, far, *parts)


def shards(inputs, cotangents, sketch_maps, lengths, queries):
    line = jnp.concatenate([queries] + [exchange(queries, 8 * d, 0) for d in (1, 2, 3)])
    sides = sides_of(inputs, cotangents, sketch_maps, lengths)
    sides, line = lax.optimization_barrier((sides, line))
    pair = jnp.concatenate([sides, exchange(sides, 0, 4)])
    parts = [pair] + [exchange(pair, 0, d) for d in (1, 2, 3)]
    lines = [line] + [exchange(line, 2 * d, 0) for d in (1, 2, 3)]
    sums = moments_of(parts)
    for d in (1, 8, 16):
        sums = sums + exchange(sums, d, 0)
    *lines, sums = lax.optimization_barrier((*lines, sums))
    sums = sums + (exchange(sums, 2, 0) + exchange(sums, 4, 0) + exchange(sums, 6, 0))
    near = jnp.concatenate(lines)
    far = exchange(near, 1, 0)
    place = jnp.stack([lax.axis_index("corpus"), lax.axis_index("query")]).astype(jnp.int32)
    return scores_of(place, sums, near, far, parts)


def solution(mesh):
    placed = (
        P(BOTH, None),
        P(BOTH, None),
        P(),
        P(BOTH),
        P(("query", "corpus"), None),
    )
    return jax.shard_map(
        shards, mesh=mesh, in_specs=placed, out_specs=P("corpus", "query"), check_vma=False
    )
```
